32 devices in a mesh: parts: 2 (over x), frame: 8 (over z, y), clip: 2 (over core).
Axes of the slice: x: 2, y: 2, z: 4, core: 2. Of those that a mesh axis runs over, the one named last changes fastest.
Arguments:
- activations: bfloat16 [4, 8, 384, 384], P(('parts', 'clip'), 'frame'), parts along dimension 0, may hold values from -6 to 6
- cotangent: bfloat16 [4, 8, 384, 384], P(('parts', 'clip'), 'frame'), parts along dimension 0, may hold values from -37 to 37
- norm_gains: float32 [3, 384], replicated, may hold values from 0.1 to 1.9
- time_input: bfloat16 [384, 1152], replicated, may hold values from -4 to 4, as said below
- time_output: bfloat16 [384, 384], replicated, may hold values from -0.3125 to 0.3125
- space_input: bfloat16 [384, 1152], replicated, may hold values from -4 to 4, as said below
- space_output: bfloat16 [384, 384], replicated, may hold values from -0.3125 to 0.3125
- hidden_up: bfloat16 [384, 1536], replicated, may hold values from -0.3125 to 0.3125
- hidden_down: bfloat16 [1536, 384], replicated, may hold values from -0.15625 to 0.15625
Outputs:
- input_grad: bfloat16 [4, 8, 384, 384], P(('parts', 'clip'), 'frame'), parts along dimension 0
- time_input_grad: float32 [768, 1152], P(('parts', 'frame')), parts along dimension 0
- time_output_grad: float32 [768, 384], P(('parts', 'frame')), parts along dimension 0
- space_input_grad: float32 [768, 1152], P(('parts', 'frame')), parts along dimension 0
- space_output_grad: float32 [768, 384], P(('parts', 'frame')), parts along dimension 0
- hidden_up_grad: float32 [768, 1536], P(('parts', 'frame')), parts along dimension 0
- hidden_down_grad: float32 [3072, 384], P(('parts', 'frame')), parts along dimension 0
- norm_gains_grad: float32 [6, 384], P('parts'), parts along dimension 0
The draws below stay inside these ranges and needn't reach their ends.
There are 2 independent parts, one for each index of `parts`. The reference program is written for one: setup_inputs(seed, part) draws one part's arguments, and reference() takes and returns one part's arrays. A program takes and returns all parts, laid end to end along the dimension named above; an argument that names none is the same for every part. Nothing has to cross between parts.
Inputs may be any that keep to these rules, and one draw needn't show every extreme that they name: `time_input`: a real-valued projection matrix. `space_input`: a real-valued projection matrix.
All inputs are finite; a program needn't handle non-finite values.
Results may differ from the reference program's by a relative error of at most 0.025.
Values may be sent and summed in bfloat16 or wider, within the bound.
No kernel may reach another device: no remote copies, remote signals or barrier semaphores. Data moves between devices by JAX's collectives and lax.ppermute only.
A program may use at most 128 MiB of HBM per device.

```python
import math
import jax
import jax.numpy as jnp
from jax import lax

D = 384
HEADS = 6
HEAD_DIM = 64
FF = 1536
PATCH = 384
FRAMES = 8
CLIPS = 2
TOKENS = 6144


def draw_cotangent(key, part):
    base_key, feature_key = jax.random.split(key, 2)
    shape = (CLIPS, FRAMES, PATCH, D)
    position = jnp.arange(FRAMES, dtype=jnp.float32) / max(FRAMES - 1, 1)
    rising = 1.0 + 2.0 * position
    feature = jnp.exp(jax.random.uniform(feature_key, (D,), jnp.float32, math.log(0.5), math.log(2.0)))
    noise = jnp.clip(jax.random.normal(base_key, shape, jnp.float32), -5.0, 5.0)
    values = noise * rising[None, :, None, None] * feature * 0.5
    return values.astype(jnp.bfloat16)


def projection_draw(key):
    base = jnp.clip(jax.random.normal(key, (D, 3, HEADS, HEAD_DIM), jnp.float32), -4.0, 4.0) / math.sqrt(D)
    return base.reshape(D, 3 * D).astype(jnp.bfloat16)


def draw_time_input(key, part):
    return projection_draw(jax.random.fold_in(key, 11))


def draw_space_input(key, part):
    return projection_draw(jax.random.fold_in(key, 23))


def shard_levels(stream_key, dims, pieces, smallest, high):
    def one(dim, parts):
        heights = jax.random.uniform(jax.random.fold_in(jax.random.fold_in(stream_key, 6), dim), (parts,), jnp.float32, smallest / len(pieces), high / len(pieces))
        return jnp.repeat(jnp.exp(heights), dims[dim] // parts).reshape((-1,) + (1,) * (len(dims) - dim - 1))

    level = one(*pieces[0])
    for cut in pieces[1:]:
        level = level * one(*cut)
    return level


def normal_values(stream_key, dims, deviation, limit, cuts=(), kind=jnp.bfloat16):
    level = shard_levels(stream_key, dims, cuts, -0.22, 0.18) if cuts else 1.0
    entries = jax.random.normal(stream_key, dims, jnp.float32) * deviation * level
    return jnp.minimum(jnp.maximum(entries, -limit), limit).astype(kind)


def setup_inputs(seed: int = 0, part: int = 0) -> dict:
    splits = jax.random.split(jax.random.key(seed), 10)
    own_keys = jax.random.split(jax.random.fold_in(splits[9], part), 10)
    return {
        "activations": normal_values(own_keys[0], (CLIPS, FRAMES, PATCH, D), 1.0, 6.0, ((0, 2), (1, 8))),
        "cotangent": draw_cotangent(jax.random.fold_in(jax.random.fold_in(splits[9], part), 71), part),
        "norm_gains": jnp.clip(1.0 + 0.18 * jax.random.normal(splits[2], (3, D), jnp.float32), 0.1, 1.9),
        "time_input": draw_time_input(jax.random.fold_in(splits[9], 71), part),
        "time_output": normal_values(splits[4], (D, D), D ** -0.5, 0.3125),
        "space_input": draw_space_input(jax.random.fold_in(splits[9], 71), part),
        "space_output": normal_values(splits[6], (D, D), D ** -0.5, 0.3125),
        "hidden_up": normal_values(splits[7], (D, FF), D ** -0.5, 0.3125),
        "hidden_down": normal_values(splits[8], (FF, D), FF ** -0.5, 0.15625),
    }


epsilon = 1e-06

def contract(form, left_op, right_op):
    return jnp.einsum(form, left_op.astype(jnp.float32), right_op.astype(jnp.float32))

def normalize(wide_rows, gain):
    center = lax.optimization_barrier(jnp.mean(wide_rows, axis=-1, keepdims=True))
    offset = wide_rows - center
    inverse = lax.rsqrt(lax.optimization_barrier(jnp.mean(offset * offset, axis=-1, keepdims=True)) + epsilon)
    normed = offset * inverse
    return ((normed * gain).astype(jnp.bfloat16), normed, inverse)

def normalize_back(hidden_grad, normed, inverse, gain):
    scaled = hidden_grad * gain
    return inverse * (scaled - lax.optimization_barrier(jnp.mean(scaled, axis=-1, keepdims=True)) - normed * lax.optimization_barrier(jnp.mean(scaled * normed, axis=-1, keepdims=True)))

def times_weight(left_rows, weight):
    flat = left_rows.reshape(-1, left_rows.shape[-1])
    result = jnp.dot(flat, weight, preferred_element_type=jnp.float32)
    return result.reshape(left_rows.shape[:-1] + (weight.shape[1],))

def times_transposed(left_rows, weight):
    flat = left_rows.reshape(-1, left_rows.shape[-1])
    result = lax.dot_general(flat, weight, (((1,), (1,)), ((), ())), preferred_element_type=jnp.float32)
    return result.reshape(left_rows.shape[:-1] + (weight.shape[0],))

def outer_sum(left_rows, right_rows):
    left_flat = left_rows.reshape(-1, left_rows.shape[-1])
    right_flat = right_rows.reshape(-1, right_rows.shape[-1])
    return lax.dot_general(left_flat, right_flat, (((0,), (0,)), ((), ())), preferred_element_type=jnp.float32)

def attention_forms(seq_first):
    if seq_first:
        return ('qbhe,kbhe->bhqk', 'bhqk,kbhe->qbhe', 'bhqk,qbhe->kbhe')
    return ('bqhe,bkhe->bhqk', 'bhqk,bkhe->bqhe', 'bhqk,bqhe->bkhe')

def split_heads(packed):
    grouped = packed.reshape(packed.shape[:-1] + (3, HEADS, packed.shape[-1] // (3 * HEADS)))
    return (grouped[..., 0, :, :], grouped[..., 1, :, :], grouped[..., 2, :, :])

def attention_shares(queries, key_rows, seq_first):
    factor = queries.shape[-1] ** (-0.5)
    scores = contract(attention_forms(seq_first)[0], queries, key_rows) * factor
    scores = scores - lax.optimization_barrier(jnp.max(scores, axis=-1, keepdims=True))
    raised = jnp.exp(scores)
    return raised / lax.optimization_barrier(jnp.sum(raised, axis=-1, keepdims=True))

def attend(packed, seq_first):
    queries, key_rows, value_rows = split_heads(packed)
    shares = attention_shares(queries, key_rows, seq_first)
    mixed = contract(attention_forms(seq_first)[1], shares.astype(jnp.bfloat16), value_rows).astype(jnp.bfloat16)
    return mixed.reshape(mixed.shape[:-2] + (-1,))

def attend_back(packed, mixed_grad, seq_first):
    score_form, out_form, back_form = attention_forms(seq_first)
    queries, key_rows, value_rows = split_heads(packed)
    grad_heads = mixed_grad.reshape(queries.shape)
    shares = attention_shares(queries, key_rows, seq_first)
    share_grad = contract(score_form, grad_heads, value_rows)
    value_grad = contract(back_form, shares.astype(jnp.bfloat16), grad_heads).astype(jnp.bfloat16)
    score_grad = shares * (share_grad - lax.optimization_barrier(jnp.sum(share_grad * shares, axis=-1, keepdims=True)))
    score_low = (score_grad * queries.shape[-1] ** (-0.5)).astype(jnp.bfloat16)
    query_grad = contract(out_form, score_low, key_rows).astype(jnp.bfloat16)
    key_grad = contract(back_form, score_low, queries).astype(jnp.bfloat16)
    stacked = jnp.stack([query_grad, key_grad, value_grad], axis=-3)
    return stacked.reshape(stacked.shape[:-3] + (-1,))

def attention_layer(rows_in, gain, in_proj, out_proj, seq_first):
    wide_rows = rows_in.astype(jnp.float32)
    hidden, normed, inverse = normalize(wide_rows, gain)
    packed = times_weight(hidden, in_proj).astype(jnp.bfloat16)
    mixed = attend(packed, seq_first)
    rows_out = (wide_rows + times_weight(mixed, out_proj)).astype(jnp.bfloat16)
    return (rows_out, (hidden, normed, inverse, packed, mixed))

def input_back(rows_grad, packed_grad, hidden, normed, inverse, gain, in_proj):
    hidden_grad = times_transposed(packed_grad, in_proj)
    gain_term = lax.optimization_barrier(jnp.sum((hidden_grad * normed).reshape(-1, hidden_grad.shape[-1]), axis=0))
    grad_in = (rows_grad.astype(jnp.float32) + normalize_back(hidden_grad, normed, inverse, gain)).astype(jnp.bfloat16)
    return (grad_in, gain_term)

def mlp_forward(rows_in, gain, up_proj):
    hidden, normed, inverse = normalize(rows_in.astype(jnp.float32), gain)
    before = times_weight(hidden, up_proj)
    active = jax.nn.gelu(before).astype(jnp.bfloat16)
    return (hidden, normed, inverse, before, active)

def mlp_back(rows_grad, saved, gain, up_proj, down_proj):
    hidden, normed, inverse, before, active = saved
    active_grad = times_transposed(rows_grad, down_proj)
    before_grad = jax.vjp(jax.nn.gelu, before)[1](active_grad)[0].astype(jnp.bfloat16)
    hidden_grad = times_transposed(before_grad, up_proj)
    gain_term = lax.optimization_barrier(jnp.sum(hidden_grad * normed, axis=0))
    grad_in = (rows_grad.astype(jnp.float32) + normalize_back(hidden_grad, normed, inverse, gain)).astype(jnp.bfloat16)
    return (grad_in, before_grad, gain_term)

def reference(activations, cotangent, norm_gains, time_input, time_output, space_input, space_output, hidden_up, hidden_down):
    clip_count, frame_count, patches, model_width = activations.shape
    factor = TOKENS ** (-0.5)
    time_rows = jnp.transpose(activations, (1, 0, 2, 3)).reshape(frame_count, clip_count * patches, model_width)
    first_time, time_saved = attention_layer(time_rows, norm_gains[0], time_input, time_output, True)
    space_rows = first_time.reshape(frame_count, clip_count, patches, model_width).transpose(1, 0, 2, 3)
    space_rows = space_rows.reshape(clip_count * frame_count, patches, model_width)

    def space_step(frame_rows):
        rows_out, saved = attention_layer(frame_rows[None], norm_gains[1], space_input, space_output, False)
        return (rows_out[0], saved)
    second_out, space_saved = lax.map(space_step, space_rows)
    flat_rows = second_out.reshape(-1, model_width)
    mlp_saved = mlp_forward(flat_rows, norm_gains[2], hidden_up)
    flat_grad = cotangent.reshape(-1, model_width)
    second_grad, before_grad, third_gain = mlp_back(flat_grad, mlp_saved, norm_gains[2], hidden_up, hidden_down)
    down_grad = outer_sum(mlp_saved[4], flat_grad) * factor
    up_grad = outer_sum(mlp_saved[0], before_grad) * factor
    frame_grads = second_grad.reshape(clip_count * frame_count, 1, patches, model_width)

    def space_back(carried):
        rows_grad, hidden, normed, inverse, packed, mixed = carried
        mixed_grad = times_transposed(rows_grad, space_output).astype(jnp.bfloat16)
        packed_grad = attend_back(packed, mixed_grad, False)
        grad_in, gain_term = input_back(rows_grad, packed_grad, hidden, normed, inverse, norm_gains[1], space_input)
        return (grad_in, packed_grad, gain_term)
    first_grad, space_packed_grad, space_gain_terms = lax.map(space_back, (frame_grads,) + tuple(space_saved))
    space_output_grad = outer_sum(space_saved[4], frame_grads) * factor
    space_input_grad = outer_sum(space_saved[0], space_packed_grad) * factor
    second_gain = lax.optimization_barrier(jnp.sum(space_gain_terms, axis=0))
    time_grad = first_grad.reshape(clip_count, frame_count, patches, model_width).transpose(1, 0, 2, 3)
    time_grad = time_grad.reshape(frame_count, clip_count * patches, model_width)
    hidden, normed, inverse, packed, mixed = time_saved
    mixed_grad = times_transposed(time_grad, time_output).astype(jnp.bfloat16)
    packed_grad = attend_back(packed, mixed_grad, True)
    time_in_rows, first_gain = input_back(time_grad, packed_grad, hidden, normed, inverse, norm_gains[0], time_input)
    time_output_grad = outer_sum(mixed, time_grad) * factor
    time_input_grad = outer_sum(hidden, packed_grad) * factor
    input_grad = time_in_rows.reshape(frame_count, clip_count, patches, model_width).transpose(1, 0, 2, 3)
    norm_gains_grad = jnp.stack([first_gain, second_gain, third_gain]) * factor
    return (input_grad, time_input_grad, time_output_grad, space_input_grad, space_output_grad, up_grad, down_grad, norm_gains_grad)
```

```python
import functools

import jax
import jax.numpy as jnp
from jax import lax
from jax.experimental import pallas as pl
from jax.experimental.pallas import tpu as pltpu
from jax.sharding import PartitionSpec as P

HEADS = 6
HEAD_DIM = 64
SCALE = HEAD_DIM ** (-0.5)
EPSILON = 1e-06
GELU_C = 0.7978845608028654
GELU_A = 0.044715
MASKED = -1e30
F32 = jnp.float32
BF16 = jnp.bfloat16


def nn(a, b):
    return lax.dot_general(a, b, (((1,), (0,)), ((), ())), preferred_element_type=F32)


def nt(a, b):
    return lax.dot_general(a, b, (((1,), (1,)), ((), ())), preferred_element_type=F32)


def tn(a, b):
    return lax.dot_general(a, b, (((0,), (0,)), ((), ())), preferred_element_type=F32)


def normalize(rows):
    offset = rows - jnp.mean(rows, axis=-1, keepdims=True)
    inverse = lax.rsqrt(jnp.mean(offset * offset, axis=-1, keepdims=True) + EPSILON)
    return offset * inverse, inverse


def normalize_back(hidden_grad, normed, inverse, gain):
    scaled = hidden_grad * gain
    return inverse * (
        scaled
        - jnp.mean(scaled, axis=-1, keepdims=True)
        - normed * jnp.mean(scaled * normed, axis=-1, keepdims=True)
    )


def lane_masks(dtype):
    lane = lax.broadcasted_iota(jnp.int32, (1, 2 * HEAD_DIM), 1)
    first = (lane < HEAD_DIM).astype(F32)
    return first.astype(dtype), (1.0 - first).astype(dtype)


def both_heads(pair):
    first, second = lane_masks(pair.dtype)
    return jnp.concatenate([pair * first, pair * second], axis=0)


def merge_heads(stacked):
    first, second = lane_masks(stacked.dtype)
    count = stacked.shape[0] // 2
    return stacked[:count] * first + stacked[count:] * second


def pair_shares(queries, keys_both, mask):
    scores = nt(queries * jnp.asarray(SCALE, BF16), keys_both)
    count = keys_both.shape[0] // 2
    shares = []
    for half in (scores[:, :count], scores[:, count:]):
        if mask is not None:
            half = jnp.where(mask, half, MASKED)
        raised = jnp.exp(half - jnp.max(half, axis=-1, keepdims=True))
        shares.append(raised * (1.0 / jnp.sum(raised, axis=-1, keepdims=True)))
    return shares


def pair_attend(queries, keys, values, mask):
    shares = pair_shares(queries, both_heads(keys), mask)
    return nn(jnp.concatenate([s.astype(BF16) for s in shares], axis=1), both_heads(values))


def pair_attend_back(queries, keys, values, mixed_grad, mask):
    keys_both = both_heads(keys)
    shares = pair_shares(queries, keys_both, mask)
    share_grad = nt(mixed_grad, both_heads(values))
    count = keys.shape[0]
    score_grads = []
    for share, grad in zip(shares, (share_grad[:, :count], share_grad[:, count:])):
        row = jnp.sum(grad * share, axis=-1, keepdims=True)
        score_grads.append((share * (grad - row) * SCALE).astype(BF16))
    score_low = jnp.concatenate(score_grads, axis=1)
    share_low = jnp.concatenate([s.astype(BF16) for s in shares], axis=1)
    query_grad = nn(score_low, keys_both)
    key_grad = merge_heads(tn(score_low, queries))
    value_grad = merge_heads(tn(share_low, mixed_grad))
    return query_grad.astype(BF16), key_grad.astype(BF16), value_grad.astype(BF16)


class Groups:
    def __init__(self, frames, share):
        self.frames, self.share = frames, share
        self.size = 16 if share % 16 == 0 else share
        self.count = share // self.size

    def mask(self):
        rows = self.frames * self.size
        i = lax.broadcasted_iota(jnp.int32, (rows, rows), 0)
        j = lax.broadcasted_iota(jnp.int32, (rows, rows), 1)
        return lax.rem(i, self.size) == lax.rem(j, self.size)

    def load(self, ref, group, first, width):
        parts = [
            ref[pl.ds(f * self.share + group * self.size, self.size), pl.ds(first, width)]
            for f in range(self.frames)
        ]
        if self.count == 1:
            return ref[:, pl.ds(first, width)]
        return jnp.concatenate(parts, axis=0)

    def store(self, ref, group, first, value):
        if self.count == 1:
            ref[:, pl.ds(first, value.shape[1])] = value
            return
        for f in range(self.frames):
            ref[pl.ds(f * self.share + group * self.size, self.size), pl.ds(first, value.shape[1])] = value[
                f * self.size : (f + 1) * self.size
            ]


def time_forward_kernel(groups, x_ref, gains_ref, in_ref, out_ref, first_ref, hidden_ref, packed_ref, mixed_ref):
    rows = x_ref[...].astype(F32)
    width = rows.shape[1]
    normed, _ = normalize(rows)
    hidden = (normed * gains_ref[0:1, :]).astype(BF16)
    hidden_ref[...] = hidden
    packed_ref[...] = nn(hidden, in_ref[...]).astype(BF16)
    mask = groups.mask()
    for group in range(groups.count):
        for first in range(0, width, 2 * HEAD_DIM):
            q, k, v = (groups.load(packed_ref, group, part * width + first, 2 * HEAD_DIM) for part in range(3))
            groups.store(mixed_ref, group, first, pair_attend(q, k, v, mask).astype(BF16))
    first_ref[...] = (rows + nn(mixed_ref[...], out_ref[...])).astype(BF16)


def store_half(core_ref, half, keep_ref, send_ref, store):
    @pl.when(core_ref[0] == half)
    def _():
        store(keep_ref)

    @pl.when(core_ref[0] != half)
    def _():
        store(send_ref)


def block_place(core_ref, owner, frames, rows, by_parity):
    if not by_parity:
        return owner * rows
    return ((owner % 2) ^ core_ref[1]) * (frames // 2 * rows) + owner // 2 * rows


def pack_columns(core_ref, frames, columns, ref, by_parity):
    share = columns[0].shape[0] // frames
    for owner in range(frames):
        place = block_place(core_ref, owner, frames, share * len(columns), by_parity)
        for index, piece in enumerate(columns):
            start = place + index * share
            if by_parity:
                start = pl.multiple_of(start, share)
            ref[pl.ds(start, share), :] = piece[owner * share : (owner + 1) * share]


def pack_rows(core_ref, frames, tall, ref):
    rows = tall.shape[0] // frames
    for owner in range(frames):
        start = pl.multiple_of(block_place(core_ref, owner, frames, rows, True), rows)
        ref[pl.ds(start, rows), :] = tall[owner * rows : (owner + 1) * rows]


def space_mlp_kernel(
    frames, factor, packed_grads,
    core_ref, x_ref, cot_ref, gains_ref, in_ref, out_ref, up_ref, down_ref,
    grad_ref, hidden_ref, packed_ref, mixed_ref, gain_ref, keep_ref, send_ref,
):
    rows = x_ref[...].astype(F32)
    width = rows.shape[1]
    normed, _ = normalize(rows)
    hidden = (normed * gains_ref[1:2, :]).astype(BF16)
    hidden_ref[...] = hidden
    packed_ref[...] = nn(hidden, in_ref[...]).astype(BF16)
    for first in range(0, width, 2 * HEAD_DIM):
        q, k, v = (packed_ref[:, pl.ds(part * width + first, 2 * HEAD_DIM)] for part in range(3))
        mixed_ref[:, pl.ds(first, 2 * HEAD_DIM)] = pair_attend(q, k, v, None).astype(BF16)
    second = (rows + nn(mixed_ref[...], out_ref[...])).astype(BF16)
    normed, inverse = normalize(second.astype(F32))
    gain = gains_ref[2:3, :]
    mlp_hidden = (normed * gain).astype(BF16)
    before = nn(mlp_hidden, up_ref[...])
    square = before * before
    bent = jnp.tanh(GELU_C * before * (1.0 + GELU_A * square))
    half_bent = 0.5 + 0.5 * bent
    active = (before * half_bent).astype(BF16)
    slope = half_bent + 0.5 * before * (1.0 - bent * bent) * (GELU_C * (1.0 + 3.0 * GELU_A * square))
    cot = cot_ref[...]
    before_grad = (slope * nt(cot, down_ref[...])).astype(BF16)
    hidden_grad = nt(before_grad, up_ref[...])
    gain_ref[...] = jnp.sum(hidden_grad * normed, axis=0, keepdims=True)
    grad_ref[...] = (cot.astype(F32) + normalize_back(hidden_grad, normed, inverse, gain)).astype(BF16)
    up_grad = (tn(mlp_hidden, before_grad) * factor).astype(BF16)
    down_grad = (tn(active, cot) * factor).astype(BF16)
    if packed_grads:
        pieces = [up_grad[:, first : first + width] for first in range(0, up_grad.shape[1], width)]
        store_half(core_ref, 0, keep_ref, send_ref, lambda ref: pack_columns(core_ref, frames, pieces, ref, True))
        store_half(core_ref, 1, keep_ref, send_ref, lambda ref: pack_rows(core_ref, frames, down_grad, ref))
    else:
        keep_ref[...] = up_grad
        send_ref[...] = down_grad


def space_back_kernel(
    x_ref, second_ref, packed_ref, gains_ref, in_ref, out_ref, grad_ref, packed_grad_ref, gain_ref
):
    second = second_ref[...]
    width = second.shape[1]
    mixed_grad = nt(second, out_ref[...]).astype(BF16)
    for first in range(0, width, 2 * HEAD_DIM):
        q, k, v = (packed_ref[:, pl.ds(part * width + first, 2 * HEAD_DIM)] for part in range(3))
        grads = pair_attend_back(q, k, v, mixed_grad[:, first : first + 2 * HEAD_DIM], None)
        for part, grad in enumerate(grads):
            packed_grad_ref[:, pl.ds(part * width + first, 2 * HEAD_DIM)] = grad
    hidden_grad = nt(packed_grad_ref[...], in_ref[...])
    normed, inverse = normalize(x_ref[...].astype(F32))
    gain_ref[...] = jnp.sum(hidden_grad * normed, axis=0, keepdims=True)
    grad_ref[...] = (
        second.astype(F32) + normalize_back(hidden_grad, normed, inverse, gains_ref[1:2, :])
    ).astype(BF16)


def store_attention_grads(core_ref, frames, packed_grads, by_parity, in_grad, out_grad, keep_ref, send_ref):
    width = out_grad.shape[1]
    if packed_grads:
        pieces = [in_grad[:, first : first + width] for first in range(0, in_grad.shape[1], width)] + [out_grad]
        for half in range(2):
            store_half(
                core_ref, half, keep_ref, send_ref,
                lambda ref, half=half: pack_columns(
                    core_ref, frames, pieces[2 * half : 2 * half + 2], ref, by_parity
                ),
            )
    else:
        keep_ref[...] = in_grad
        send_ref[...] = out_grad


def space_weights_kernel(
    frames, factor, packed_grads, core_ref, hidden_ref, packed_grad_ref, mixed_ref, second_ref, keep_ref, send_ref
):
    in_grad = (tn(hidden_ref[...], packed_grad_ref[...]) * factor).astype(BF16)
    out_grad = (tn(mixed_ref[...], second_ref[...]) * factor).astype(BF16)
    store_attention_grads(core_ref, frames, packed_grads, True, in_grad, out_grad, keep_ref, send_ref)


def time_back_kernel(
    groups, factor, packed_grads,
    core_ref, grad_ref, hidden_ref, packed_ref, mixed_ref, out_ref,
    packed_grad_ref, keep_ref, send_ref, mixed_grad_ref,
):
    grad = grad_ref[...]
    width = grad.shape[1]
    mixed_grad_ref[...] = nt(grad, out_ref[...]).astype(BF16)
    mask = groups.mask()
    for group in range(groups.count):
        for first in range(0, width, 2 * HEAD_DIM):
            q, k, v = (groups.load(packed_ref, group, part * width + first, 2 * HEAD_DIM) for part in range(3))
            grads = pair_attend_back(q, k, v, groups.load(mixed_grad_ref, group, first, 2 * HEAD_DIM), mask)
            for part, value in enumerate(grads):
                groups.store(packed_grad_ref, group, part * width + first, value)
    in_grad = (tn(hidden_ref[...], packed_grad_ref[...]) * factor).astype(BF16)
    out_grad = (tn(mixed_ref[...], grad) * factor).astype(BF16)
    store_attention_grads(core_ref, groups.frames, packed_grads, False, in_grad, out_grad, keep_ref, send_ref)


def time_input_kernel(x_ref, grad_ref, packed_grad_ref, gains_ref, in_ref, input_ref, gain_ref):
    hidden_grad = nt(packed_grad_ref[...], in_ref[...])
    normed, inverse = normalize(x_ref[...].astype(F32))
    gain_ref[...] = jnp.sum(hidden_grad * normed, axis=0, keepdims=True)
    input_ref[...] = (
        grad_ref[...].astype(F32) + normalize_back(hidden_grad, normed, inverse, gains_ref[0:1, :])
    ).astype(BF16)


def call(kernel, outs, args, scalars=0, scratch=(), flops=0, name=None):
    vmem = pl.BlockSpec(memory_space=pltpu.VMEM)
    specs = [pl.BlockSpec(memory_space=pltpu.SMEM)] * scalars + [vmem] * (len(args) - scalars)
    return pl.pallas_call(
        kernel,
        out_shape=[jax.ShapeDtypeStruct(shape, dtype) for shape, dtype in outs],
        in_specs=specs,
        out_specs=[vmem] * len(outs),
        scratch_shapes=list(scratch),
        compiler_params=pltpu.CompilerParams(vmem_limit_bytes=40 * 1024 * 1024),
        cost_estimate=pl.CostEstimate(flops=flops, transcendentals=0, bytes_accessed=4000000),
        name=name,
    )(*args)


def natural_halves(core, frames, by_parity, first, second):
    width = min(first.shape[1], second.shape[1])

    def blocks(matrix):
        matrix = matrix.reshape(frames, matrix.shape[0] // frames, -1, width)
        return jnp.swapaxes(matrix, 1, 2).reshape(frames, -1, width)

    first, second = blocks(first), blocks(second)
    if first.shape != second.shape:
        whole = jnp.concatenate([first, second], axis=1)
        middle = whole.shape[1] // 2
        first, second = whole[:, :middle], whole[:, middle:]
    if by_parity:

        def order(blocked):
            blocked = jnp.swapaxes(blocked.reshape((frames // 2, 2) + blocked.shape[1:]), 0, 1)
            return jnp.where(core[1] == 0, blocked, blocked[::-1]).reshape((frames,) + blocked.shape[2:])

        first, second = order(first), order(second)
    swap = core[0] == 0
    return jnp.where(swap, first, second), jnp.where(swap, second, first)


def swap_clips(array):
    return lax.ppermute(array, "clip", [(0, 1), (1, 0)])


def summed(*terms):
    total = terms[0].astype(F32)
    for term in terms[1:]:
        total = total + term.astype(F32)
    return total


def reduce_by_parity(keep, send, frames):
    half = frames // 2
    keep = keep.reshape(2, half, -1, keep.shape[-1])
    got = swap_clips(send).reshape(keep.shape)
    other = summed(keep[1], got[1]).astype(BF16)
    near = lax.ppermute(other, "frame", [(i, i ^ 1) for i in range(frames)])
    mine = summed(keep[0], got[0], near).astype(BF16)
    groups = [list(range(parity, frames, 2)) for parity in range(2)]
    terms = lax.all_to_all(mine, "frame", split_axis=0, concat_axis=0, tiled=True, axis_index_groups=groups)
    return jnp.sum(terms.astype(F32), axis=0).astype(BF16)


def side_by_side(stacked, count):
    share = stacked.shape[0] // count
    return jnp.concatenate([stacked[i * share : (i + 1) * share] for i in range(count)], axis=1)


def exchange(rows, frames):
    blocks = rows.reshape(frames, -1, rows.shape[-1])
    return lax.all_to_all(blocks, "frame", split_axis=0, concat_axis=0, tiled=True)


def body(
    activations,
    cotangent,
    norm_gains,
    time_input,
    time_output,
    space_input,
    space_output,
    hidden_up,
    hidden_down,
):
    frames = lax.axis_size("frame")
    tokens, width = activations.shape[2], activations.shape[3]
    share = tokens // frames
    packed = share % 16 == 0
    tokens_all = tokens * frames * lax.axis_size("clip")
    factor = tokens_all ** (-0.5)
    groups = Groups(frames, share)
    core = jnp.stack([lax.axis_index("clip"), lax.axis_index("frame") % 2]).astype(jnp.int32)
    rows_bf = ((tokens, width), BF16)
    wide_bf = ((tokens, time_input.shape[1]), BF16)
    gain_f32 = ((1, width), F32)
    if packed:
        attention_terms = [((2 * width, width), BF16)] * 2
        mlp_terms = [((hidden_down.shape[0], width), BF16)] * 2
    else:
        attention_terms = [(time_input.shape, BF16), (time_output.shape, BF16)]
        mlp_terms = [(hidden_up.shape, BF16), (hidden_down.shape, BF16)]

    def halves(keep, send, by_parity):
        if packed:
            return (x.reshape(frames, -1, width) for x in (keep, send))
        return natural_halves(core, frames, by_parity, keep, send)

    cot = cotangent.reshape(tokens, width)
    patch_rows = exchange(activations.reshape(tokens, width), frames).reshape(tokens, width)
    first_patch, time_hidden, time_packed, time_mixed = call(
        functools.partial(time_forward_kernel, groups),
        [rows_bf, rows_bf, wide_bf, rows_bf],
        [patch_rows, norm_gains, time_input, time_output],
        flops=10**9,
        name="time_forward",
    )
    first_out = exchange(first_patch, frames).reshape(tokens, width)
    second_grad, space_hidden, space_packed, space_mixed, third_gain, mlp_keep, mlp_send = call(
        functools.partial(space_mlp_kernel, frames, factor, packed),
        [rows_bf, rows_bf, wide_bf, rows_bf, gain_f32] + mlp_terms,
        [core, first_out, cot, norm_gains, space_input, space_output, hidden_up, hidden_down],
        scalars=1,
        flops=4 * 10**9,
        name="space_mlp",
    )
    mlp_keep, mlp_send = halves(mlp_keep, mlp_send, True)
    first_grad, space_packed_grad, second_gain = call(
        space_back_kernel,
        [rows_bf, wide_bf, gain_f32],
        [first_out, second_grad, space_packed, norm_gains, space_input, space_output],
        flops=3 * 10**9,
        name="space_back",
    )
    patch_grad = exchange(first_grad, frames).reshape(tokens, width)
    space_keep, space_send = call(
        functools.partial(space_weights_kernel, frames, factor, packed),
        attention_terms,
        [core, space_hidden, space_packed_grad, space_mixed, second_grad],
        scalars=1,
        flops=10**9,
        name="space_weights",
    )
    space_keep, space_send = halves(space_keep, space_send, True)
    time_packed_grad, time_keep, time_send = call(
        functools.partial(time_back_kernel, groups, factor, packed),
        [wide_bf] + attention_terms,
        [core, patch_grad, time_hidden, time_packed, time_mixed, time_output],
        scalars=1,
        scratch=[pltpu.VMEM((tokens, width), BF16)],
        flops=2 * 10**9,
        name="time_back",
    )
    time_keep, time_send = halves(time_keep, time_send, False)
    input_patch, first_gain = call(
        time_input_kernel,
        [rows_bf, gain_f32],
        [patch_rows, patch_grad, time_packed_grad, norm_gains, time_input],
        flops=10**9,
        name="time_input",
    )

    mlp_own = reduce_by_parity(mlp_keep, mlp_send, frames)
    space_own = reduce_by_parity(space_keep, space_send, frames)

    gains = jnp.concatenate([first_gain, second_gain, third_gain], axis=0) * factor
    gains_high = gains.astype(BF16)
    gains_low = (gains - gains_high.astype(F32)).astype(BF16)
    gain_rows = jnp.concatenate([gains_high, gains_low, jnp.zeros((10, width), BF16)], axis=0)
    time_terms = summed(time_keep, swap_clips(time_send)).astype(BF16)
    last = jnp.concatenate(
        [
            time_terms,
            input_patch.reshape(frames, share, width),
            jnp.broadcast_to(gain_rows[None], (frames,) + gain_rows.shape),
        ],
        axis=1,
    )
    last = lax.all_to_all(last, "frame", split_axis=0, concat_axis=0, tiled=True)
    input_grad = last[:, 2 * share : 3 * share].reshape(activations.shape)
    time_own = jnp.sum(last[:, : 2 * share].astype(F32), axis=0).astype(BF16)
    gains_sum = jnp.sum(last[:, 3 * share :].astype(F32), axis=0)
    gains_sum = gains_sum[:3] + gains_sum[3:6]
    sum_high = gains_sum.astype(BF16)
    sum_low = (gains_sum - sum_high.astype(F32)).astype(BF16)

    own = jnp.concatenate([mlp_own, space_own], axis=0)
    got = swap_clips(own)
    tail_own = jnp.concatenate([time_own, sum_high, sum_low], axis=0)
    tail_got = swap_clips(tail_own)
    mlp_rows = mlp_own.shape[0]

    def both(mine, theirs):
        lead = core[0] == 0
        return jnp.where(lead, mine, theirs).astype(F32), jnp.where(lead, theirs, mine).astype(F32)

    up_rows, down_rows = both(own[:mlp_rows], got[:mlp_rows])
    up_grad = side_by_side(up_rows, hidden_up.shape[1] // width)

    def attention_out(mine, theirs):
        lower, upper = both(mine, theirs)
        in_grad = jnp.concatenate([lower[:share], lower[share:], upper[:share]], axis=1)
        return in_grad, upper[share:]

    space_in_grad, space_out_grad = attention_out(own[mlp_rows:], got[mlp_rows:])
    time_in_grad, time_out_grad = attention_out(tail_own[: 2 * share], tail_got[: 2 * share])
    gains_own, gains_got = tail_own[2 * share :].astype(F32), tail_got[2 * share :].astype(F32)
    gains_grad = (gains_own[:3] + gains_own[3:]) + (gains_got[:3] + gains_got[3:])
    return (
        input_grad,
        time_in_grad,
        time_out_grad,
        space_in_grad,
        space_out_grad,
        up_grad,
        down_rows,
        gains_grad,
    )


def solution(mesh):
    tokens = P(("parts", "clip"), "frame", None, None)
    owned = P(("parts", "frame"), None)
    in_specs = (tokens, tokens) + (P(),) * 7
    out_specs = (tokens,) + (owned,) * 6 + (P("parts", None),)
    return jax.shard_map(body, mesh=mesh, in_specs=in_specs, out_specs=out_specs, check_vma=False)
```

```python
import functools

import jax
import jax.numpy as jnp
from jax import lax
from jax.experimental import pallas as pl
from jax.experimental.pallas import tpu as pltpu
from jax.sharding import PartitionSpec as P

HEADS = 6
HEAD_DIM = 64
SCALE = HEAD_DIM ** (-0.5)
EPSILON = 1e-06
GELU_C = 0.7978845608028654
GELU_A = 0.044715
MASKED = -1e30
F32 = jnp.float32
BF16 = jnp.bfloat16


def nn(a, b):
    return lax.dot_general(a, b, (((1,), (0,)), ((), ())), preferred_element_type=F32)


def nt(a, b):
    return lax.dot_general(a, b, (((1,), (1,)), ((), ())), preferred_element_type=F32)


def tn(a, b):
    return lax.dot_general(a, b, (((0,), (0,)), ((), ())), preferred_element_type=F32)


def normalize(rows):
    offset = rows - jnp.mean(rows, axis=-1, keepdims=True)
    inverse = lax.rsqrt(jnp.mean(offset * offset, axis=-1, keepdims=True) + EPSILON)
    return offset * inverse, inverse


def normalize_back(hidden_grad, normed, inverse, gain):
    scaled = hidden_grad * gain
    return inverse * (
        scaled
        - jnp.mean(scaled, axis=-1, keepdims=True)
        - normed * jnp.mean(scaled * normed, axis=-1, keepdims=True)
    )


def lane_masks(dtype):
    lane = lax.broadcasted_iota(jnp.int32, (1, 2 * HEAD_DIM), 1)
    first = (lane < HEAD_DIM).astype(F32)
    return first.astype(dtype), (1.0 - first).astype(dtype)


def both_heads(pair):
    first, second = lane_masks(pair.dtype)
    return jnp.concatenate([pair * first, pair * second], axis=0)


def merge_heads(stacked):
    first, second = lane_masks(stacked.dtype)
    count = stacked.shape[0] // 2
    return stacked[:count] * first + stacked[count:] * second


def pair_attend(queries, keys, values, mask):
    scores = nt(both_heads(keys), queries * jnp.asarray(SCALE, BF16))
    count = keys.shape[0]
    shares = []
    for half in (scores[:count], scores[count:]):
        if mask is not None:
            half = jnp.where(mask, half, MASKED)
        raised = jnp.exp(half - jnp.max(half, axis=0, keepdims=True))
        shares.append((raised * (1.0 / jnp.sum(raised, axis=0, keepdims=True))).astype(BF16))
    shares = jnp.concatenate(shares, axis=0)
    return tn(shares, both_heads(values)).astype(BF16), shares


def pair_attend_back(queries, keys, values, mixed_grad, shares):
    count = keys.shape[0]
    share_grad = nt(both_heads(values), mixed_grad)
    score_grads = []
    for start in (0, count):
        share = shares[start : start + count].astype(F32)
        grad = share_grad[start : start + count]
        row = jnp.sum(grad * share, axis=0, keepdims=True)
        score_grads.append((share * (grad - row) * SCALE).astype(BF16))
    score_grad = jnp.concatenate(score_grads, axis=0)
    query_grad = tn(score_grad, both_heads(keys))
    key_grad = merge_heads(nn(score_grad, queries))
    value_grad = merge_heads(nn(shares, mixed_grad))
    return query_grad.astype(BF16), key_grad.astype(BF16), value_grad.astype(BF16)


class Groups:
    def __init__(self, frames, share):
        self.frames, self.share = frames, share
        self.size = 16 if share % 16 == 0 else share
        self.count = share // self.size

    def mask(self):
        rows = self.frames * self.size
        i = lax.broadcasted_iota(jnp.int32, (rows, rows), 0)
        j = lax.broadcasted_iota(jnp.int32, (rows, rows), 1)
        return lax.rem(i, self.size) == lax.rem(j, self.size)

    def load(self, ref, group, first, width):
        parts = [
            ref[pl.ds(f * self.share + group * self.size, self.size), pl.ds(first, width)]
            for f in range(self.frames)
        ]
        if self.count == 1:
            return ref[:, pl.ds(first, width)]
        return jnp.concatenate(parts, axis=0)

    def store(self, ref, group, first, value):
        if self.count == 1:
            ref[:, pl.ds(first, value.shape[1])] = value
            return
        for f in range(self.frames):
            ref[pl.ds(f * self.share + group * self.size, self.size), pl.ds(first, value.shape[1])] = value[
                f * self.size : (f + 1) * self.size
            ]


def active_grad_kernel(cot_ref, down_ref, grad_ref):
    grad_ref[...] = nt(cot_ref[...], down_ref[...])


def time_forward_kernel(
    groups, x_ref, gains_ref, in_ref, out_ref, first_ref, hidden_ref, packed_ref, mixed_ref, shares_ref
):
    rows = x_ref[...].astype(F32)
    width = rows.shape[1]
    normed, _ = normalize(rows)
    hidden = (normed * gains_ref[0:1, :]).astype(BF16)
    hidden_ref[...] = hidden
    packed_ref[...] = nn(hidden, in_ref[...]).astype(BF16)
    mask = groups.mask()
    block = 0
    for group in range(groups.count):
        for first in range(0, width, 2 * HEAD_DIM):
            q, k, v = (groups.load(packed_ref, group, part * width + first, 2 * HEAD_DIM) for part in range(3))
            mixed, shares = pair_attend(q, k, v, mask)
            groups.store(mixed_ref, group, first, mixed)
            shares_ref[pl.ds(block, shares.shape[0]), :] = shares
            block += shares.shape[0]
    send(hidden_ref, packed_ref, mixed_ref, shares_ref)
    first_ref[...] = (rows + nn(mixed_ref[...], out_ref[...])).astype(BF16)


def store_half(core_ref, half, keep_ref, send_ref, store):
    @pl.when(core_ref[0] == half)
    def _():
        store(keep_ref)

    @pl.when(core_ref[0] != half)
    def _():
        store(send_ref)


def fold_bits(frames):
    return list(range(frames.bit_length() - 1))


def fold_place(apart, frames):
    bits = fold_bits(frames)
    place = 0
    for index, bit in enumerate(bits):
        place = place + (((apart >> bit) & 1) << (len(bits) - 1 - index))
    return place


def block_place(core_ref, owner, frames, rows, folded):
    if not folded:
        return owner * rows
    return pl.multiple_of(fold_place(owner ^ core_ref[1], frames) * rows, rows)


def pack_columns(core_ref, frames, columns, ref, folded):
    share = columns[0].shape[0] // frames
    for owner in range(frames):
        place = block_place(core_ref, owner, frames, share * len(columns), folded)
        for index, piece in enumerate(columns):
            start = place + index * share
            if folded:
                start = pl.multiple_of(start, share)
            ref[pl.ds(start, share), :] = piece[owner * share : (owner + 1) * share]


def pack_rows(core_ref, frames, tall, ref):
    rows = tall.shape[0] // frames
    for owner in range(frames):
        start = block_place(core_ref, owner, frames, rows, True)
        ref[pl.ds(start, rows), :] = tall[owner * rows : (owner + 1) * rows]


def space_mlp_kernel(
    frames, factor, packed_grads,
    core_ref, x_ref, cot_ref, gains_ref, in_ref, out_ref, up_ref, active_grad_ref,
    grad_ref, hidden_ref, packed_ref, mixed_ref, shares_ref, gain_ref, keep_ref, send_ref,
):
    rows = x_ref[...].astype(F32)
    width = rows.shape[1]
    normed, _ = normalize(rows)
    hidden = (normed * gains_ref[1:2, :]).astype(BF16)
    hidden_ref[...] = hidden
    packed_ref[...] = nn(hidden, in_ref[...]).astype(BF16)
    for first in range(0, width, 2 * HEAD_DIM):
        q, k, v = (packed_ref[:, pl.ds(part * width + first, 2 * HEAD_DIM)] for part in range(3))
        mixed, shares = pair_attend(q, k, v, None)
        mixed_ref[:, pl.ds(first, 2 * HEAD_DIM)] = mixed
        shares_ref[pl.ds(first // (2 * HEAD_DIM) * shares.shape[0], shares.shape[0]), :] = shares
    second = (rows + nn(mixed_ref[...], out_ref[...])).astype(BF16)
    normed, inverse = normalize(second.astype(F32))
    gain = gains_ref[2:3, :]
    mlp_hidden = (normed * gain).astype(BF16)
    before = nn(mlp_hidden, up_ref[...])
    square = before * before
    bent = jnp.tanh(GELU_C * before * (1.0 + GELU_A * square))
    half_bent = 0.5 + 0.5 * bent
    active = (before * half_bent).astype(BF16)
    slope = half_bent + 0.5 * before * (1.0 - bent * bent) * (GELU_C * (1.0 + 3.0 * GELU_A * square))
    cot = cot_ref[...]
    before_grad = (slope * active_grad_ref[...]).astype(BF16)
    hidden_grad = nt(before_grad, up_ref[...])
    gain_ref[...] = jnp.sum(hidden_grad * normed, axis=0, keepdims=True)
    send(hidden_ref, mixed_ref, gain_ref)
    grad_ref[...] = (cot.astype(F32) + normalize_back(hidden_grad, normed, inverse, gain)).astype(BF16)
    up_grad = (tn(mlp_hidden, before_grad) * factor).astype(BF16)
    down_grad = (tn(active, cot) * factor).astype(BF16)
    if packed_grads:
        pieces = [up_grad[:, first : first + width] for first in range(0, up_grad.shape[1], width)]
        store_half(core_ref, 0, keep_ref, send_ref, lambda ref: pack_columns(core_ref, frames, pieces, ref, True))
        store_half(core_ref, 1, keep_ref, send_ref, lambda ref: pack_rows(core_ref, frames, down_grad, ref))
    else:
        keep_ref[...] = up_grad
        send_ref[...] = down_grad


def space_back_kernel(
    x_ref, second_ref, packed_ref, shares_ref, gains_ref, in_ref, out_ref, grad_ref, packed_grad_ref, gain_ref
):
    second = second_ref[...]
    width = second.shape[1]
    mixed_grad = nt(second, out_ref[...]).astype(BF16)
    for first in range(0, width, 2 * HEAD_DIM):
        q, k, v = (packed_ref[:, pl.ds(part * width + first, 2 * HEAD_DIM)] for part in range(3))
        start = first // (2 * HEAD_DIM) * 2 * second.shape[0]
        shares = shares_ref[pl.ds(start, 2 * second.shape[0]), :]
        grads = pair_attend_back(q, k, v, mixed_grad[:, first : first + 2 * HEAD_DIM], shares)
        for part, grad in enumerate(grads):
            packed_grad_ref[:, pl.ds(part * width + first, 2 * HEAD_DIM)] = grad
    send(packed_grad_ref)
    hidden_grad = nt(packed_grad_ref[...], in_ref[...])
    normed, inverse = normalize(x_ref[...].astype(F32))
    gain_ref[...] = jnp.sum(hidden_grad * normed, axis=0, keepdims=True)
    grad_ref[...] = (
        second.astype(F32) + normalize_back(hidden_grad, normed, inverse, gains_ref[1:2, :])
    ).astype(BF16)


def store_attention_grads(core_ref, frames, packed_grads, folded, in_grad, out_grad, keep_ref, send_ref):
    width = out_grad.shape[1]
    if packed_grads:
        pieces = [in_grad[:, first : first + width] for first in range(0, in_grad.shape[1], width)] + [out_grad]
        for half in range(2):
            store_half(
                core_ref, half, keep_ref, send_ref,
                lambda ref, half=half: pack_columns(
                    core_ref, frames, pieces[2 * half : 2 * half + 2], ref, folded
                ),
            )
    else:
        keep_ref[...] = in_grad
        send_ref[...] = out_grad


def space_weights_kernel(
    frames, factor, packed_grads, core_ref, hidden_ref, packed_grad_ref, mixed_ref, second_ref, keep_ref, send_ref
):
    in_grad = (tn(hidden_ref[...], packed_grad_ref[...]) * factor).astype(BF16)
    out_grad = (tn(mixed_ref[...], second_ref[...]) * factor).astype(BF16)
    store_attention_grads(core_ref, frames, packed_grads, True, in_grad, out_grad, keep_ref, send_ref)


def time_back_kernel(
    groups, factor, packed_grads,
    core_ref, grad_ref, hidden_ref, packed_ref, mixed_ref, shares_ref, out_ref,
    packed_grad_ref, keep_ref, send_ref, mixed_grad_ref,
):
    grad = grad_ref[...]
    width = grad.shape[1]
    mixed_grad_ref[...] = nt(grad, out_ref[...]).astype(BF16)
    rows = 2 * groups.frames * groups.size
    block = 0
    for group in range(groups.count):
        for first in range(0, width, 2 * HEAD_DIM):
            q, k, v = (groups.load(packed_ref, group, part * width + first, 2 * HEAD_DIM) for part in range(3))
            part_grad = groups.load(mixed_grad_ref, group, first, 2 * HEAD_DIM)
            grads = pair_attend_back(q, k, v, part_grad, shares_ref[pl.ds(block, rows), :])
            block += rows
            for part, value in enumerate(grads):
                groups.store(packed_grad_ref, group, part * width + first, value)
    in_grad = (tn(hidden_ref[...], packed_grad_ref[...]) * factor).astype(BF16)
    out_grad = (tn(mixed_ref[...], grad) * factor).astype(BF16)
    store_attention_grads(core_ref, groups.frames, packed_grads, False, in_grad, out_grad, keep_ref, send_ref)


def time_input_kernel(x_ref, grad_ref, packed_grad_ref, gains_ref, in_ref, input_ref, gain_ref):
    hidden_grad = nt(packed_grad_ref[...], in_ref[...])
    normed, inverse = normalize(x_ref[...].astype(F32))
    gain_ref[...] = jnp.sum(hidden_grad * normed, axis=0, keepdims=True)
    input_ref[...] = (
        grad_ref[...].astype(F32) + normalize_back(hidden_grad, normed, inverse, gains_ref[0:1, :])
    ).astype(BF16)


class Arriving:
    def __init__(self, source, target, semaphore):
        self.target, self.copy = target, pltpu.make_async_copy(source, target, semaphore)
        self.copy.start()
        self.waited = False

    def wait(self):
        if not self.waited:
            self.copy.wait()
            self.waited = True

    def __getitem__(self, index):
        self.wait()
        return self.target[index]


class Leaving:
    def __init__(self, source, target, semaphore):
        self.source, self.copy = source, pltpu.make_async_copy(source, target, semaphore)
        self.sent = False

    def send(self):
        if not self.sent:
            self.copy.start()
            self.sent = True

    def __getitem__(self, index):
        return self.source[index]

    def __setitem__(self, index, value):
        self.source[index] = value


def send(*refs):
    for ref in refs:
        if isinstance(ref, Leaving):
            ref.send()


def call(kernel, outs, args, scalars=0, scratch=(), vmem=16, name=None, far_in=(), far_out=()):
    near, far = pl.BlockSpec(memory_space=pltpu.VMEM), pl.BlockSpec(memory_space=pltpu.HBM)
    in_specs = [pl.BlockSpec(memory_space=pltpu.SMEM)] * scalars
    in_specs += [far if i in far_in else near for i in range(scalars, len(args))]
    staging = [pltpu.VMEM(args[i].shape, args[i].dtype) for i in far_in]
    staging += [pltpu.VMEM(*outs[i]) for i in far_out]
    count = len(args) + len(outs)

    def staged(*refs):
        refs, extra, stages, semaphores = (
            list(refs[:count]),
            refs[count : count + len(scratch)],
            refs[count + len(scratch) : count + len(scratch) + len(staging)],
            refs[-1],
        )
        leaving = []
        for k, i in enumerate(far_in):
            refs[i] = Arriving(refs[i], stages[k], semaphores.at[k])
        for k, i in enumerate(far_out):
            k += len(far_in)
            refs[len(args) + i] = Leaving(stages[k], refs[len(args) + i], semaphores.at[k])
            leaving.append(refs[len(args) + i])
        kernel(*refs, *extra)
        for i in far_in:
            refs[i].wait()
        for ref in leaving:
            ref.send()
        for ref in leaving:
            ref.copy.wait()

    args = [pltpu.with_memory_space_constraint(a, pltpu.HBM) if i in far_in else a for i, a in enumerate(args)]
    return pl.pallas_call(
        staged,
        out_shape=[
            pltpu.HBM(shape, dtype) if i in far_out else jax.ShapeDtypeStruct(shape, dtype)
            for i, (shape, dtype) in enumerate(outs)
        ],
        in_specs=in_specs,
        out_specs=[far if i in far_out else near for i in range(len(outs))],
        scratch_shapes=list(scratch) + staging + [pltpu.SemaphoreType.DMA((max(len(staging), 1),))],
        compiler_params=pltpu.CompilerParams(vmem_limit_bytes=vmem * 1024 * 1024),
        cost_estimate=CHEAP,
        name=name,
    )(*args)


def prefetch_kernel(count, *refs):
    sources, targets, semaphores = refs[:count], refs[count : 2 * count], refs[-1]
    copies = [pltpu.make_async_copy(sources[i], targets[i], semaphores.at[i]) for i in range(count)]
    for copy in copies:
        copy.start()
    for copy in copies:
        copy.wait()


def prefetch(*arrays):
    return pl.pallas_call(
        functools.partial(prefetch_kernel, len(arrays)),
        out_shape=[pltpu.VMEM(a.shape, a.dtype) for a in arrays],
        in_specs=[pl.BlockSpec(memory_space=pltpu.HBM)] * len(arrays),
        out_specs=[pl.BlockSpec(memory_space=pltpu.VMEM)] * len(arrays),
        scratch_shapes=[pltpu.SemaphoreType.DMA((len(arrays),))],
        compiler_params=pltpu.CompilerParams(vmem_limit_bytes=1024 * 1024),
        cost_estimate=CHEAP,
        name="prefetch",
    )(*[pltpu.with_memory_space_constraint(a, pltpu.HBM) for a in arrays])


def natural_halves(core, frames, folded, first, second):
    width = min(first.shape[1], second.shape[1])

    def blocks(matrix):
        matrix = matrix.reshape(frames, matrix.shape[0] // frames, -1, width)
        return jnp.swapaxes(matrix, 1, 2).reshape(frames, -1, width)

    first, second = blocks(first), blocks(second)
    if first.shape != second.shape:
        whole = jnp.concatenate([first, second], axis=1)
        middle = whole.shape[1] // 2
        first, second = whole[:, :middle], whole[:, middle:]
    if folded:
        places = jnp.stack([fold_place(jnp.int32(owner) ^ core[1], frames) for owner in range(frames)])
        first, second = (jnp.zeros_like(blocked).at[places].set(blocked) for blocked in (first, second))
    swap = core[0] == 0
    return jnp.where(swap, first, second), jnp.where(swap, second, first)


def swap_clips(array):
    return lax.ppermute(array, "clip", [(0, 1), (1, 0)])


CHEAP = pl.CostEstimate(flops=1000, transcendentals=0, bytes_accessed=1000)


def sum_kernel(*refs):
    total = refs[0][...].astype(F32)
    for ref in refs[1:-1]:
        total = total + ref[...].astype(F32)
    refs[-1][...] = total.astype(BF16)


def block_sum(terms, count, place):
    shape = (count,) + terms[0].shape[1:]
    return pl.pallas_call(
        sum_kernel,
        grid=(1,),
        out_shape=jax.ShapeDtypeStruct(shape, BF16),
        in_specs=[pl.BlockSpec(shape, lambda i: (place, 0, 0))] * len(terms),
        out_specs=pl.BlockSpec(shape, lambda i: (0, 0, 0)),
        compiler_params=pltpu.CompilerParams(vmem_limit_bytes=16 * 1024 * 1024),
        cost_estimate=CHEAP,
        name="block_sum",
    )(*terms)


def fold_send(terms):
    half = terms[-1].shape[0] // 2
    return block_sum(terms, half, 1)


def fold(terms, bit, frames, send=None):
    send = fold_send(terms) if send is None else send
    return terms + [lax.ppermute(send, "frame", [(i, i ^ (1 << bit)) for i in range(frames)])]


def own_sum(terms):
    return block_sum(terms, 1, 0)[0]


def two_parts(values):
    high = values.astype(BF16).astype(F32)
    zeros = jnp.zeros((10, values.shape[1]), F32)
    return jnp.concatenate([high, values - high, zeros], axis=0).astype(BF16)


def unpack_kernel(terms, last_ref, own_ref, rows_ref):
    share = rows_ref.shape[1]
    own_ref[pl.ds(0, terms), :] = jnp.sum(last_ref[:, pl.ds(0, terms), :].astype(F32), axis=0).astype(BF16)
    gains = jnp.sum(last_ref[:, pl.ds(terms + share, 16), :].astype(F32), axis=0)
    own_ref[pl.ds(terms, 16), :] = two_parts(gains[:3] + gains[3:6])
    rows_ref[...] = last_ref[:, pl.ds(terms, share), :]


def pack_kernel(factor, keep_ref, got_ref, rows_ref, first_ref, second_ref, third_ref, last_ref):
    terms, share = keep_ref.shape[1], rows_ref.shape[1]
    last_ref[:, pl.ds(0, terms), :] = (keep_ref[...].astype(F32) + got_ref[...].astype(F32)).astype(BF16)
    last_ref[:, pl.ds(terms, share), :] = rows_ref[...]
    gains = jnp.concatenate([first_ref[...], second_ref[...], third_ref[...]], axis=0) * factor
    block, width = two_parts(gains), rows_ref.shape[2]
    last_ref[:, pl.ds(terms + share, 16), :] = jnp.broadcast_to(block[None], (keep_ref.shape[0], 16, width))


def finish_kernel(layout, gains, core_ref, own_ref, got_ref, *out_refs):
    if gains is not None:
        pair = [ref[pl.ds(gains, 16), :].astype(F32) for ref in (own_ref, got_ref)]
        out_refs[-1][...] = (pair[0][:3] + pair[0][3:6]) + (pair[1][:3] + pair[1][3:6])

    def store(first_ref, second_ref):
        for half, start, rows, width, out, column in layout:
            piece = (first_ref, second_ref)[half][pl.ds(start, rows), :]
            out_refs[out][:, pl.ds(column, width)] = piece.astype(F32)

    @pl.when(core_ref[0] == 0)
    def _():
        store(own_ref, got_ref)

    @pl.when(core_ref[0] != 0)
    def _():
        store(got_ref, own_ref)


def finish(packed, core, own, got, outs, layout, name, gains=None):
    if packed:
        outs = outs if gains is None else outs + [((3, own.shape[1]), F32)]
        return call(functools.partial(finish_kernel, layout, gains), outs, [core, own, got], scalars=1, vmem=12, name=name)
    pair = jnp.where(core[0] == 0, own, got), jnp.where(core[0] == 0, got, own)
    results = []
    for out in range(len(outs)):
        pieces = [pair[half][start : start + rows] for half, start, rows, _, to, _ in layout if to == out]
        results.append(jnp.concatenate(pieces, axis=1).astype(F32))
    if gains is not None:
        first, second = (x[gains : gains + 6].astype(F32) for x in (own, got))
        results.append((first[:3] + first[3:]) + (second[:3] + second[3:]))
    return results


def exchange(rows, frames):
    blocks = rows.reshape(frames, -1, rows.shape[-1])
    return lax.all_to_all(blocks, "frame", split_axis=0, concat_axis=0, tiled=True)


def body(
    activations,
    cotangent,
    norm_gains,
    time_input,
    time_output,
    space_input,
    space_output,
    hidden_up,
    hidden_down,
):
    frames = lax.axis_size("frame")
    tokens, width = activations.shape[2], activations.shape[3]
    inner = hidden_down.shape[0]
    share = tokens // frames
    packed = share % 16 == 0
    factor = (tokens * frames * lax.axis_size("clip")) ** (-0.5)
    groups = Groups(frames, share)
    group_rows = frames * groups.size
    core = jnp.stack([lax.axis_index("clip"), lax.axis_index("frame")]).astype(jnp.int32)
    rows_bf = ((tokens, width), BF16)
    wide_bf = ((tokens, time_input.shape[1]), BF16)
    gain_f32 = ((1, width), F32)
    if packed:
        attention_terms = [((2 * width, width), BF16)] * 2
        mlp_terms = [((inner, width), BF16)] * 2
    else:
        attention_terms = [(time_input.shape, BF16), (time_output.shape, BF16)]
        mlp_terms = [(hidden_up.shape, BF16), (hidden_down.shape, BF16)]

    def halves(keep, send, folded):
        if packed:
            return [x.reshape(frames, -1, width) for x in (keep, send)]
        return natural_halves(core, frames, folded, keep, send)

    cot = cotangent.reshape(tokens, width)
    patch_rows = exchange(activations.reshape(tokens, width), frames).reshape(tokens, width)
    first_gain_row, time_in, time_out = prefetch(norm_gains, time_input, time_output)
    gain_rows, space_in, space_out = prefetch(norm_gains, space_input, space_output)
    (active_grad,) = call(
        active_grad_kernel, [((tokens, inner), F32)], [cot, hidden_down], vmem=16, name="active_grad", far_in=(0, 1), far_out=(0,)
    )
    first_patch, time_hidden, time_packed, time_mixed, time_shares = call(
        functools.partial(time_forward_kernel, groups),
        [rows_bf, rows_bf, wide_bf, rows_bf, ((width * tokens // HEAD_DIM, group_rows), BF16)],
        [patch_rows, first_gain_row, time_in, time_out],
        vmem=20,
        name="time_forward",
        far_out=(1, 2, 3, 4),
    )
    first_out = exchange(first_patch, frames).reshape(tokens, width)
    second_grad, space_hidden, space_packed, space_mixed, space_shares, third_gain, mlp_keep, mlp_send = call(
        functools.partial(space_mlp_kernel, frames, factor, packed),
        [rows_bf, rows_bf, wide_bf, rows_bf, ((width * tokens // HEAD_DIM, tokens), BF16), gain_f32] + mlp_terms,
        [core, first_out, cot, gain_rows, space_in, space_out, hidden_up, active_grad],
        scalars=1,
        vmem=36,
        name="space_mlp",
        far_in=(2, 6, 7),
        far_out=(1, 3, 5, 6),
    )
    mlp_keep, mlp_send = halves(mlp_keep, mlp_send, True)
    mlp_terms = [mlp_keep, swap_clips(mlp_send)]
    first_grad, space_packed_grad, second_gain = call(
        space_back_kernel,
        [rows_bf, wide_bf, gain_f32],
        [first_out, second_grad, space_packed, space_shares, gain_rows, space_in, space_out],
        vmem=24,
        name="space_back",
        far_out=(1, 2),
    )
    patch_grad = exchange(first_grad, frames).reshape(tokens, width)
    space_keep, space_send = call(
        functools.partial(space_weights_kernel, frames, factor, packed),
        attention_terms,
        [core, space_hidden, space_packed_grad, space_mixed, second_grad],
        scalars=1,
        vmem=20,
        name="space_weights",
        far_in=(1, 2, 3, 4),
        far_out=(0,),
    )
    space_keep, space_send = halves(space_keep, space_send, True)
    bits = fold_bits(frames)
    mlp_send, space_keep, patch_grad = lax.optimization_barrier((fold_send(mlp_terms), space_keep, patch_grad))
    mlp_terms = fold(mlp_terms, bits[0], frames, mlp_send)
    time_packed_grad, time_keep, time_send = call(
        functools.partial(time_back_kernel, groups, factor, packed),
        [wide_bf] + attention_terms,
        [core, patch_grad, time_hidden, time_packed, time_mixed, time_shares, time_output],
        scalars=1,
        scratch=[pltpu.VMEM((tokens, width), BF16)],
        vmem=24,
        name="time_back",
        far_in=(3, 6, 5, 2, 4),
    )
    time_keep, time_send = halves(time_keep, time_send, False)
    time_got = swap_clips(time_send)
    space_terms = [space_keep, swap_clips(space_send)]
    input_patch, first_gain = call(
        time_input_kernel,
        [rows_bf, gain_f32],
        [patch_rows, patch_grad, time_packed_grad, norm_gains, time_input],
        vmem=16,
        name="time_input",
        far_in=(4, 0),
    )
    space_sum, mlp_terms[-1], time_keep = lax.optimization_barrier(
        (fold_send(space_terms), mlp_terms[-1], time_keep)
    )
    space_terms = fold(space_terms, bits[0], frames, space_sum)
    mlp_terms = fold(mlp_terms, bits[1], frames)

    (last,) = call(
        functools.partial(pack_kernel, factor),
        [((frames, 3 * share + 16, width), BF16)],
        [time_keep, time_got, input_patch.reshape(frames, share, width), first_gain, second_gain, third_gain],
        vmem=16,
        name="pack",
        far_out=(0,),
    )
    last = lax.all_to_all(last, "frame", split_axis=0, concat_axis=0, tiled=True)
    late_own, input_grad = call(
        functools.partial(unpack_kernel, 2 * share),
        [((2 * share + 16, width), BF16), ((frames, share, width), BF16)],
        [last],
        vmem=16,
        name="unpack",
    )
    input_grad = input_grad.reshape(activations.shape)

    for bit in bits[1:]:
        space_terms = fold(space_terms, bit, frames)
    for bit in bits[2:]:
        mlp_terms = fold(mlp_terms, bit, frames)
    early_own = jnp.concatenate([own_sum(mlp_terms), own_sum(space_terms)], axis=0)
    early_got = swap_clips(early_own)
    late_got = swap_clips(late_own)

    mlp_rows = inner // frames
    attention_layout = [(0, 0, 0, 0), (0, 1, 0, width), (1, 0, 0, 2 * width), (1, 1, 1, 0)]
    early_layout = [(0, i * share, share, width, 0, i * width) for i in range(inner // width)]
    early_layout += [(1, 0, mlp_rows, width, 1, 0)]
    early_layout += [
        (half, mlp_rows + index * share, share, width, 2 + out, column)
        for half, index, out, column in attention_layout
    ]
    late_layout = [(half, index * share, share, width, out, column) for half, index, out, column in attention_layout]
    attention_outs = [((share, time_input.shape[1]), F32), ((share, width), F32)]
    mlp_outs = [((share, inner), F32), ((mlp_rows, width), F32)]
    up_grad, down_grad, space_in_grad, space_out_grad = finish(
        packed, core, early_own, early_got, mlp_outs + attention_outs, early_layout, "finish_early"
    )
    time_in_grad, time_out_grad, gains_grad = finish(
        packed, core, late_own, late_got, attention_outs, late_layout, "finish_late", gains=2 * share
    )
    return (
        input_grad,
        time_in_grad,
        time_out_grad,
        space_in_grad,
        space_out_grad,
        up_grad,
        down_grad,
        gains_grad,
    )


def solution(mesh):
    tokens = P(("parts", "clip"), "frame", None, None)
    owned = P(("parts", "frame"), None)
    in_specs = (tokens, tokens) + (P(),) * 7
    out_specs = (tokens,) + (owned,) * 6 + (P("parts", None),)
    return jax.shard_map(body, mesh=mesh, in_specs=in_specs, out_specs=out_specs, check_vma=False)
```

```python
import functools

import jax
import jax.numpy as jnp
from jax import lax
from jax.experimental import pallas as pl
from jax.experimental.pallas import tpu as pltpu
from jax.sharding import PartitionSpec as P

HEADS = 6
HEAD_DIM = 64
SCALE = HEAD_DIM ** (-0.5)
EPSILON = 1e-06
GELU_C = 0.7978845608028654
GELU_A = 0.044715
MASKED = -1e30
F32 = jnp.float32
BF16 = jnp.bfloat16


def nn(a, b):
    return lax.dot_general(a, b, (((1,), (0,)), ((), ())), preferred_element_type=F32)


def nt(a, b):
    return lax.dot_general(a, b, (((1,), (1,)), ((), ())), preferred_element_type=F32)


def tn(a, b):
    return lax.dot_general(a, b, (((0,), (0,)), ((), ())), preferred_element_type=F32)


def normalize(rows):
    offset = rows - jnp.mean(rows, axis=-1, keepdims=True)
    inverse = lax.rsqrt(jnp.mean(offset * offset, axis=-1, keepdims=True) + EPSILON)
    return offset * inverse, inverse


def normalize_back(hidden_grad, normed, inverse, gain):
    scaled = hidden_grad * gain
    return inverse * (
        scaled
        - jnp.mean(scaled, axis=-1, keepdims=True)
        - normed * jnp.mean(scaled * normed, axis=-1, keepdims=True)
    )


def lane_masks(dtype):
    lane = lax.broadcasted_iota(jnp.int32, (1, 2 * HEAD_DIM), 1)
    first = (lane < HEAD_DIM).astype(F32)
    return first.astype(dtype), (1.0 - first).astype(dtype)


def both_heads(pair):
    first, second = lane_masks(pair.dtype)
    return jnp.concatenate([pair * first, pair * second], axis=0)


def merge_heads(stacked):
    first, second = lane_masks(stacked.dtype)
    count = stacked.shape[0] // 2
    return stacked[:count] * first + stacked[count:] * second


def pair_attend(queries, keys, values, mask):
    scores = nt(both_heads(keys), queries * jnp.asarray(SCALE, BF16))
    count = keys.shape[0]
    shares = []
    for half in (scores[:count], scores[count:]):
        if mask is not None:
            half = jnp.where(mask, half, MASKED)
        raised = jnp.exp(half - jnp.max(half, axis=0, keepdims=True))
        shares.append((raised * (1.0 / jnp.sum(raised, axis=0, keepdims=True))).astype(BF16))
    shares = jnp.concatenate(shares, axis=0)
    return tn(shares, both_heads(values)).astype(BF16), shares


def pair_attend_back(queries, keys, values, mixed_grad, shares):
    count = keys.shape[0]
    share_grad = nt(both_heads(values), mixed_grad)
    score_grads = []
    for start in (0, count):
        share = shares[start : start + count].astype(F32)
        grad = share_grad[start : start + count]
        row = jnp.sum(grad * share, axis=0, keepdims=True)
        score_grads.append((share * (grad - row) * SCALE).astype(BF16))
    score_grad = jnp.concatenate(score_grads, axis=0)
    query_grad = tn(score_grad, both_heads(keys))
    key_grad = merge_heads(nn(score_grad, queries))
    value_grad = merge_heads(nn(shares, mixed_grad))
    return query_grad.astype(BF16), key_grad.astype(BF16), value_grad.astype(BF16)


class Groups:
    def __init__(self, frames, share):
        self.frames, self.share = frames, share
        self.size = 16 if share % 16 == 0 else share
        self.count = share // self.size

    def mask(self):
        rows = self.frames * self.size
        i = lax.broadcasted_iota(jnp.int32, (rows, rows), 0)
        j = lax.broadcasted_iota(jnp.int32, (rows, rows), 1)
        return lax.rem(i, self.size) == lax.rem(j, self.size)

    def load(self, ref, group, first, width):
        parts = [
            ref[pl.ds(f * self.share + group * self.size, self.size), pl.ds(first, width)]
            for f in range(self.frames)
        ]
        if self.count == 1:
            return ref[:, pl.ds(first, width)]
        return jnp.concatenate(parts, axis=0)

    def store(self, ref, group, first, value):
        if self.count == 1:
            ref[:, pl.ds(first, value.shape[1])] = value
            return
        for f in range(self.frames):
            ref[pl.ds(f * self.share + group * self.size, self.size), pl.ds(first, value.shape[1])] = value[
                f * self.size : (f + 1) * self.size
            ]


def active_grad_kernel(cot_ref, down_ref, grad_ref):
    grad_ref[...] = nt(cot_ref[...], down_ref[...])


def time_forward_kernel(
    groups, x_ref, gains_ref, in_ref, out_ref, first_ref, hidden_ref, packed_ref, mixed_ref, shares_ref
):
    rows = x_ref[...].astype(F32)
    width = rows.shape[1]
    normed, _ = normalize(rows)
    hidden = (normed * gains_ref[0:1, :]).astype(BF16)
    hidden_ref[...] = hidden
    packed_ref[...] = nn(hidden, in_ref[...]).astype(BF16)
    send(hidden_ref, packed_ref)
    mask = groups.mask()
    block = 0
    for group in range(groups.count):
        for first in range(0, width, 2 * HEAD_DIM):
            q, k, v = (groups.load(packed_ref, group, part * width + first, 2 * HEAD_DIM) for part in range(3))
            mixed, shares = pair_attend(q, k, v, mask)
            groups.store(mixed_ref, group, first, mixed)
            shares_ref[pl.ds(block, shares.shape[0]), :] = shares
            block += shares.shape[0]
    send(mixed_ref, shares_ref)
    first_ref[...] = (rows + nn(mixed_ref[...], out_ref[...])).astype(BF16)


def store_half(core_ref, half, keep_ref, send_ref, store):
    @pl.when(core_ref[0] == half)
    def _():
        store(keep_ref)

    @pl.when(core_ref[0] != half)
    def _():
        store(send_ref)


def fold_bits(frames):
    return list(range(frames.bit_length() - 1))


def fold_place(apart, frames):
    bits = fold_bits(frames)
    place = 0
    for index, bit in enumerate(bits):
        place = place + (((apart >> bit) & 1) << (len(bits) - 1 - index))
    return place


def block_place(core_ref, owner, frames, rows, folded):
    if not folded:
        return owner * rows
    return pl.multiple_of(fold_place(owner ^ core_ref[1], frames) * rows, rows)


def pack_columns(core_ref, frames, columns, ref, folded):
    share = columns[0].shape[0] // frames
    for owner in range(frames):
        place = block_place(core_ref, owner, frames, share * len(columns), folded)
        for index, piece in enumerate(columns):
            start = place + index * share
            if folded:
                start = pl.multiple_of(start, share)
            ref[pl.ds(start, share), :] = piece[owner * share : (owner + 1) * share]


def pack_rows(core_ref, frames, tall, ref):
    rows = tall.shape[0] // frames
    for owner in range(frames):
        start = block_place(core_ref, owner, frames, rows, True)
        ref[pl.ds(start, rows), :] = tall[owner * rows : (owner + 1) * rows]


def space_mlp_kernel(
    frames, factor, packed_grads,
    core_ref, x_ref, cot_ref, gains_ref, in_ref, out_ref, up_ref, active_grad_ref,
    grad_ref, hidden_ref, packed_ref, mixed_ref, shares_ref, gain_ref, keep_ref, send_ref,
):
    rows = x_ref[...].astype(F32)
    width = rows.shape[1]
    normed, _ = normalize(rows)
    hidden = (normed * gains_ref[1:2, :]).astype(BF16)
    hidden_ref[...] = hidden
    packed_ref[...] = nn(hidden, in_ref[...]).astype(BF16)
    for first in range(0, width, 2 * HEAD_DIM):
        q, k, v = (packed_ref[:, pl.ds(part * width + first, 2 * HEAD_DIM)] for part in range(3))
        mixed, shares = pair_attend(q, k, v, None)
        mixed_ref[:, pl.ds(first, 2 * HEAD_DIM)] = mixed
        shares_ref[pl.ds(first // (2 * HEAD_DIM) * shares.shape[0], shares.shape[0]), :] = shares
    second = (rows + nn(mixed_ref[...], out_ref[...])).astype(BF16)
    normed, inverse = normalize(second.astype(F32))
    gain = gains_ref[2:3, :]
    mlp_hidden = (normed * gain).astype(BF16)
    before = nn(mlp_hidden, up_ref[...])
    square = before * before
    bent = jnp.tanh(GELU_C * before * (1.0 + GELU_A * square))
    half_bent = 0.5 + 0.5 * bent
    active = (before * half_bent).astype(BF16)
    slope = half_bent + 0.5 * before * (1.0 - bent * bent) * (GELU_C * (1.0 + 3.0 * GELU_A * square))
    cot = cot_ref[...]
    before_grad = (slope * active_grad_ref[...]).astype(BF16)
    hidden_grad = nt(before_grad, up_ref[...])
    gain_ref[...] = jnp.sum(hidden_grad * normed, axis=0, keepdims=True)
    send(hidden_ref, mixed_ref, gain_ref)
    grad_ref[...] = (cot.astype(F32) + normalize_back(hidden_grad, normed, inverse, gain)).astype(BF16)
    up_grad = (tn(mlp_hidden, before_grad) * factor).astype(BF16)
    down_grad = (tn(active, cot) * factor).astype(BF16)
    if packed_grads:
        pieces = [up_grad[:, first : first + width] for first in range(0, up_grad.shape[1], width)]
        store_half(core_ref, 0, keep_ref, send_ref, lambda ref: pack_columns(core_ref, frames, pieces, ref, True))
        store_half(core_ref, 1, keep_ref, send_ref, lambda ref: pack_rows(core_ref, frames, down_grad, ref))
    else:
        keep_ref[...] = up_grad
        send_ref[...] = down_grad


def space_back_kernel(
    x_ref, second_ref, packed_ref, shares_ref, gains_ref, in_ref, out_ref, grad_ref, packed_grad_ref, gain_ref
):
    second = second_ref[...]
    width = second.shape[1]
    mixed_grad = nt(second, out_ref[...]).astype(BF16)
    for first in range(0, width, 2 * HEAD_DIM):
        q, k, v = (packed_ref[:, pl.ds(part * width + first, 2 * HEAD_DIM)] for part in range(3))
        start = first // (2 * HEAD_DIM) * 2 * second.shape[0]
        shares = shares_ref[pl.ds(start, 2 * second.shape[0]), :]
        grads = pair_attend_back(q, k, v, mixed_grad[:, first : first + 2 * HEAD_DIM], shares)
        for part, grad in enumerate(grads):
            packed_grad_ref[:, pl.ds(part * width + first, 2 * HEAD_DIM)] = grad
    send(packed_grad_ref)
    hidden_grad = nt(packed_grad_ref[...], in_ref[...])
    normed, inverse = normalize(x_ref[...].astype(F32))
    gain_ref[...] = jnp.sum(hidden_grad * normed, axis=0, keepdims=True)
    grad_ref[...] = (
        second.astype(F32) + normalize_back(hidden_grad, normed, inverse, gains_ref[1:2, :])
    ).astype(BF16)


def store_attention_grads(core_ref, frames, packed_grads, folded, in_grad, out_grad, keep_ref, send_ref):
    width = out_grad.shape[1]
    if packed_grads:
        pieces = [in_grad[:, first : first + width] for first in range(0, in_grad.shape[1], width)] + [out_grad]
        for half in range(2):
            store_half(
                core_ref, half, keep_ref, send_ref,
                lambda ref, half=half: pack_columns(
                    core_ref, frames, pieces[2 * half : 2 * half + 2], ref, folded
                ),
            )
    else:
        keep_ref[...] = in_grad
        send_ref[...] = out_grad


def space_weights_kernel(
    frames, factor, packed_grads, core_ref, hidden_ref, packed_grad_ref, mixed_ref, second_ref, keep_ref, send_ref
):
    in_grad = (tn(hidden_ref[...], packed_grad_ref[...]) * factor).astype(BF16)
    out_grad = (tn(mixed_ref[...], second_ref[...]) * factor).astype(BF16)
    store_attention_grads(core_ref, frames, packed_grads, True, in_grad, out_grad, keep_ref, send_ref)


def time_back_kernel(
    groups, factor, packed_grads,
    core_ref, grad_ref, hidden_ref, packed_ref, mixed_ref, shares_ref, out_ref,
    packed_grad_ref, keep_ref, send_ref, mixed_grad_ref,
):
    grad = grad_ref[...]
    width = grad.shape[1]
    mixed_grad_ref[...] = nt(grad, out_ref[...]).astype(BF16)
    rows = 2 * groups.frames * groups.size
    block = 0
    for group in range(groups.count):
        for first in range(0, width, 2 * HEAD_DIM):
            q, k, v = (groups.load(packed_ref, group, part * width + first, 2 * HEAD_DIM) for part in range(3))
            part_grad = groups.load(mixed_grad_ref, group, first, 2 * HEAD_DIM)
            grads = pair_attend_back(q, k, v, part_grad, shares_ref[pl.ds(block, rows), :])
            block += rows
            for part, value in enumerate(grads):
                groups.store(packed_grad_ref, group, part * width + first, value)
    in_grad = (tn(hidden_ref[...], packed_grad_ref[...]) * factor).astype(BF16)
    out_grad = (tn(mixed_ref[...], grad) * factor).astype(BF16)
    store_attention_grads(core_ref, groups.frames, packed_grads, False, in_grad, out_grad, keep_ref, send_ref)


def time_input_kernel(x_ref, grad_ref, packed_grad_ref, gains_ref, in_ref, input_ref, gain_ref):
    hidden_grad = nt(packed_grad_ref[...], in_ref[...])
    normed, inverse = normalize(x_ref[...].astype(F32))
    gain_ref[...] = jnp.sum(hidden_grad * normed, axis=0, keepdims=True)
    input_ref[...] = (
        grad_ref[...].astype(F32) + normalize_back(hidden_grad, normed, inverse, gains_ref[0:1, :])
    ).astype(BF16)


class Arriving:
    def __init__(self, source, target, semaphore):
        self.target, self.copy = target, pltpu.make_async_copy(source, target, semaphore)
        self.copy.start()
        self.waited = False

    def wait(self):
        if not self.waited:
            self.copy.wait()
            self.waited = True

    def __getitem__(self, index):
        self.wait()
        return self.target[index]


class Leaving:
    def __init__(self, source, target, semaphore):
        self.source, self.copy = source, pltpu.make_async_copy(source, target, semaphore)
        self.sent = False

    def send(self):
        if not self.sent:
            self.copy.start()
            self.sent = True

    def __getitem__(self, index):
        return self.source[index]

    def __setitem__(self, index, value):
        self.source[index] = value


def send(*refs):
    for ref in refs:
        if isinstance(ref, Leaving):
            ref.send()


def call(kernel, outs, args, scalars=0, scratch=(), vmem=16, name=None, far_in=(), far_out=()):
    near, far = pl.BlockSpec(memory_space=pltpu.VMEM), pl.BlockSpec(memory_space=pltpu.HBM)
    in_specs = [pl.BlockSpec(memory_space=pltpu.SMEM)] * scalars
    in_specs += [far if i in far_in else near for i in range(scalars, len(args))]
    staging = [pltpu.VMEM(args[i].shape, args[i].dtype) for i in far_in]
    staging += [pltpu.VMEM(*outs[i]) for i in far_out]
    count = len(args) + len(outs)

    def staged(*refs):
        refs, extra, stages, semaphores = (
            list(refs[:count]),
            refs[count : count + len(scratch)],
            refs[count + len(scratch) : count + len(scratch) + len(staging)],
            refs[-1],
        )
        leaving = []
        for k, i in enumerate(far_in):
            refs[i] = Arriving(refs[i], stages[k], semaphores.at[k])
        for k, i in enumerate(far_out):
            k += len(far_in)
            refs[len(args) + i] = Leaving(stages[k], refs[len(args) + i], semaphores.at[k])
            leaving.append(refs[len(args) + i])
        kernel(*refs, *extra)
        for i in far_in:
            refs[i].wait()
        for ref in leaving:
            ref.send()
        for ref in leaving:
            ref.copy.wait()

    args = [pltpu.with_memory_space_constraint(a, pltpu.HBM) if i in far_in else a for i, a in enumerate(args)]
    return pl.pallas_call(
        staged,
        out_shape=[
            pltpu.HBM(shape, dtype) if i in far_out else jax.ShapeDtypeStruct(shape, dtype)
            for i, (shape, dtype) in enumerate(outs)
        ],
        in_specs=in_specs,
        out_specs=[far if i in far_out else near for i in range(len(outs))],
        scratch_shapes=list(scratch) + staging + [pltpu.SemaphoreType.DMA((max(len(staging), 1),))],
        compiler_params=pltpu.CompilerParams(vmem_limit_bytes=vmem * 1024 * 1024),
        cost_estimate=CHEAP,
        name=name,
    )(*args)


def prefetch_kernel(count, *refs):
    sources, targets, semaphores = refs[:count], refs[count : 2 * count], refs[-1]
    copies = [pltpu.make_async_copy(sources[i], targets[i], semaphores.at[i]) for i in range(count)]
    for copy in copies:
        copy.start()
    for copy in copies:
        copy.wait()


def prefetch(*arrays):
    return pl.pallas_call(
        functools.partial(prefetch_kernel, len(arrays)),
        out_shape=[pltpu.VMEM(a.shape, a.dtype) for a in arrays],
        in_specs=[pl.BlockSpec(memory_space=pltpu.HBM)] * len(arrays),
        out_specs=[pl.BlockSpec(memory_space=pltpu.VMEM)] * len(arrays),
        scratch_shapes=[pltpu.SemaphoreType.DMA((len(arrays),))],
        compiler_params=pltpu.CompilerParams(vmem_limit_bytes=1024 * 1024),
        cost_estimate=CHEAP,
        name="prefetch",
    )(*[pltpu.with_memory_space_constraint(a, pltpu.HBM) for a in arrays])


def natural_halves(core, frames, folded, first, second):
    width = min(first.shape[1], second.shape[1])

    def blocks(matrix):
        matrix = matrix.reshape(frames, matrix.shape[0] // frames, -1, width)
        return jnp.swapaxes(matrix, 1, 2).reshape(frames, -1, width)

    first, second = blocks(first), blocks(second)
    if first.shape != second.shape:
        whole = jnp.concatenate([first, second], axis=1)
        middle = whole.shape[1] // 2
        first, second = whole[:, :middle], whole[:, middle:]
    if folded:
        places = jnp.stack([fold_place(jnp.int32(owner) ^ core[1], frames) for owner in range(frames)])
        first, second = (jnp.zeros_like(blocked).at[places].set(blocked) for blocked in (first, second))
    swap = core[0] == 0
    return jnp.where(swap, first, second), jnp.where(swap, second, first)


def swap_clips(array):
    return lax.ppermute(array, "clip", [(0, 1), (1, 0)])


CHEAP = pl.CostEstimate(flops=1000, transcendentals=0, bytes_accessed=1000)


def sum_kernel(*refs):
    total = refs[0][...].astype(F32)
    for ref in refs[1:-1]:
        total = total + ref[...].astype(F32)
    refs[-1][...] = total.astype(BF16)


def block_sum(terms, count, place):
    shape = (count,) + terms[0].shape[1:]
    return pl.pallas_call(
        sum_kernel,
        grid=(1,),
        out_shape=jax.ShapeDtypeStruct(shape, BF16),
        in_specs=[pl.BlockSpec(shape, lambda i: (place, 0, 0))] * len(terms),
        out_specs=pl.BlockSpec(shape, lambda i: (0, 0, 0)),
        compiler_params=pltpu.CompilerParams(vmem_limit_bytes=16 * 1024 * 1024),
        cost_estimate=CHEAP,
        name="block_sum",
    )(*terms)


def fold_send(terms):
    half = terms[-1].shape[0] // 2
    return block_sum(terms, half, 1)


def fold(terms, bit, frames, send=None):
    send = fold_send(terms) if send is None else send
    return terms + [lax.ppermute(send, "frame", [(i, i ^ (1 << bit)) for i in range(frames)])]


def own_sum(terms):
    return block_sum(terms, 1, 0)[0]


def two_parts(values):
    high = values.astype(BF16).astype(F32)
    zeros = jnp.zeros((10, values.shape[1]), F32)
    return jnp.concatenate([high, values - high, zeros], axis=0).astype(BF16)


def unpack_kernel(terms, last_ref, own_ref, rows_ref):
    share = rows_ref.shape[1]
    own_ref[pl.ds(0, terms), :] = jnp.sum(last_ref[:, pl.ds(0, terms), :].astype(F32), axis=0).astype(BF16)
    gains = jnp.sum(last_ref[:, pl.ds(terms + share, 16), :].astype(F32), axis=0)
    own_ref[pl.ds(terms, 16), :] = two_parts(gains[:3] + gains[3:6])
    rows_ref[...] = last_ref[:, pl.ds(terms, share), :]


def pack_kernel(factor, keep_ref, got_ref, rows_ref, first_ref, second_ref, third_ref, last_ref):
    terms, share = keep_ref.shape[1], rows_ref.shape[1]
    last_ref[:, pl.ds(0, terms), :] = (keep_ref[...].astype(F32) + got_ref[...].astype(F32)).astype(BF16)
    last_ref[:, pl.ds(terms, share), :] = rows_ref[...]
    gains = jnp.concatenate([first_ref[...], second_ref[...], third_ref[...]], axis=0) * factor
    block, width = two_parts(gains), rows_ref.shape[2]
    last_ref[:, pl.ds(terms + share, 16), :] = jnp.broadcast_to(block[None], (keep_ref.shape[0], 16, width))


def finish_kernel(layout, gains, core_ref, own_ref, got_ref, *out_refs):
    if gains is not None:
        pair = [ref[pl.ds(gains, 16), :].astype(F32) for ref in (own_ref, got_ref)]
        out_refs[-1][...] = (pair[0][:3] + pair[0][3:6]) + (pair[1][:3] + pair[1][3:6])

    def store(first_ref, second_ref):
        for half, start, rows, width, out, column in layout:
            piece = (first_ref, second_ref)[half][pl.ds(start, rows), :]
            out_refs[out][:, pl.ds(column, width)] = piece.astype(F32)

    @pl.when(core_ref[0] == 0)
    def _():
        store(own_ref, got_ref)

    @pl.when(core_ref[0] != 0)
    def _():
        store(got_ref, own_ref)


def finish(packed, core, own, got, outs, layout, name, gains=None):
    if packed:
        outs = outs if gains is None else outs + [((3, own.shape[1]), F32)]
        return call(functools.partial(finish_kernel, layout, gains), outs, [core, own, got], scalars=1, vmem=12, name=name)
    pair = jnp.where(core[0] == 0, own, got), jnp.where(core[0] == 0, got, own)
    results = []
    for out in range(len(outs)):
        pieces = [pair[half][start : start + rows] for half, start, rows, _, to, _ in layout if to == out]
        results.append(jnp.concatenate(pieces, axis=1).astype(F32))
    if gains is not None:
        first, second = (x[gains : gains + 6].astype(F32) for x in (own, got))
        results.append((first[:3] + first[3:]) + (second[:3] + second[3:]))
    return results


def exchange(rows, frames):
    blocks = rows.reshape(frames, -1, rows.shape[-1])
    return lax.all_to_all(blocks, "frame", split_axis=0, concat_axis=0, tiled=True)


def body(
    activations,
    cotangent,
    norm_gains,
    time_input,
    time_output,
    space_input,
    space_output,
    hidden_up,
    hidden_down,
):
    frames = lax.axis_size("frame")
    tokens, width = activations.shape[2], activations.shape[3]
    inner = hidden_down.shape[0]
    share = tokens // frames
    packed = share % 16 == 0
    factor = (tokens * frames * lax.axis_size("clip")) ** (-0.5)
    groups = Groups(frames, share)
    group_rows = frames * groups.size
    core = jnp.stack([lax.axis_index("clip"), lax.axis_index("frame")]).astype(jnp.int32)
    rows_bf = ((tokens, width), BF16)
    wide_bf = ((tokens, time_input.shape[1]), BF16)
    gain_f32 = ((1, width), F32)
    if packed:
        attention_terms = [((2 * width, width), BF16)] * 2
        mlp_terms = [((inner, width), BF16)] * 2
    else:
        attention_terms = [(time_input.shape, BF16), (time_output.shape, BF16)]
        mlp_terms = [(hidden_up.shape, BF16), (hidden_down.shape, BF16)]

    def halves(keep, send, folded):
        if packed:
            return [x.reshape(frames, -1, width) for x in (keep, send)]
        return natural_halves(core, frames, folded, keep, send)

    cot = cotangent.reshape(tokens, width)
    patch_rows = exchange(activations.reshape(tokens, width), frames).reshape(tokens, width)
    first_gain_row, time_in, time_out = prefetch(norm_gains, time_input, time_output)
    gain_rows, space_in, space_out = prefetch(norm_gains, space_input, space_output)
    (active_grad,) = call(
        active_grad_kernel, [((tokens, inner), F32)], [cot, hidden_down], vmem=16, name="active_grad", far_in=(0, 1), far_out=(0,)
    )
    first_patch, time_hidden, time_packed, time_mixed, time_shares = call(
        functools.partial(time_forward_kernel, groups),
        [rows_bf, rows_bf, wide_bf, rows_bf, ((width * tokens // HEAD_DIM, group_rows), BF16)],
        [patch_rows, first_gain_row, time_in, time_out],
        vmem=20,
        name="time_forward",
        far_out=(1, 2, 3, 4),
    )
    first_out = exchange(first_patch, frames).reshape(tokens, width)
    second_grad, space_hidden, space_packed, space_mixed, space_shares, third_gain, mlp_keep, mlp_send = call(
        functools.partial(space_mlp_kernel, frames, factor, packed),
        [rows_bf, rows_bf, wide_bf, rows_bf, ((width * tokens // HEAD_DIM, tokens), BF16), gain_f32] + mlp_terms,
        [core, first_out, cot, gain_rows, space_in, space_out, hidden_up, active_grad],
        scalars=1,
        vmem=36,
        name="space_mlp",
        far_in=(2, 6, 7),
        far_out=(1, 3, 5),
    )
    mlp_keep, mlp_send = halves(mlp_keep, mlp_send, True)
    mlp_terms = [mlp_keep, swap_clips(mlp_send)]
    first_grad, space_packed_grad, second_gain = call(
        space_back_kernel,
        [rows_bf, wide_bf, gain_f32],
        [first_out, second_grad, space_packed, space_shares, gain_rows, space_in, space_out],
        vmem=24,
        name="space_back",
        far_out=(1, 2),
    )
    patch_grad = exchange(first_grad, frames).reshape(tokens, width)
    space_keep, space_send = call(
        functools.partial(space_weights_kernel, frames, factor, packed),
        attention_terms,
        [core, space_hidden, space_packed_grad, space_mixed, second_grad],
        scalars=1,
        vmem=20,
        name="space_weights",
        far_in=(1, 2, 3, 4),
        far_out=(0,),
    )
    space_keep, space_send = halves(space_keep, space_send, True)
    bits = fold_bits(frames)
    mlp_send, space_keep, patch_grad = lax.optimization_barrier((fold_send(mlp_terms), space_keep, patch_grad))
    mlp_terms = fold(mlp_terms, bits[0], frames, mlp_send)
    time_packed_grad, time_keep, time_send = call(
        functools.partial(time_back_kernel, groups, factor, packed),
        [wide_bf] + attention_terms,
        [core, patch_grad, time_hidden, time_packed, time_mixed, time_shares, time_output],
        scalars=1,
        scratch=[pltpu.VMEM((tokens, width), BF16)],
        vmem=24,
        name="time_back",
        far_in=(3, 6, 5, 2, 4),
    )
    time_keep, time_send = halves(time_keep, time_send, False)
    time_got = swap_clips(time_send)
    space_terms = [space_keep, swap_clips(space_send)]
    input_patch, first_gain = call(
        time_input_kernel,
        [rows_bf, gain_f32],
        [patch_rows, patch_grad, time_packed_grad, norm_gains, time_input],
        vmem=16,
        name="time_input",
        far_in=(4, 0),
    )
    space_sum, mlp_terms[-1], time_keep = lax.optimization_barrier(
        (fold_send(space_terms), mlp_terms[-1], time_keep)
    )
    space_terms = fold(space_terms, bits[0], frames, space_sum)
    mlp_terms = fold(mlp_terms, bits[1], frames)

    (last,) = call(
        functools.partial(pack_kernel, factor),
        [((frames, 3 * share + 16, width), BF16)],
        [time_keep, time_got, input_patch.reshape(frames, share, width), first_gain, second_gain, third_gain],
        vmem=16,
        name="pack",
        far_out=(0,),
    )
    last = lax.all_to_all(last, "frame", split_axis=0, concat_axis=0, tiled=True)
    late_own, input_grad = call(
        functools.partial(unpack_kernel, 2 * share),
        [((2 * share + 16, width), BF16), ((frames, share, width), BF16)],
        [last],
        vmem=16,
        name="unpack",
    )
    input_grad = input_grad.reshape(activations.shape)

    for bit in bits[1:]:
        space_terms = fold(space_terms, bit, frames)
    for bit in bits[2:]:
        mlp_terms = fold(mlp_terms, bit, frames)
    early_own = jnp.concatenate([own_sum(mlp_terms), own_sum(space_terms)], axis=0)
    early_got = swap_clips(early_own)
    late_got = swap_clips(late_own)

    mlp_rows = inner // frames
    attention_layout = [(0, 0, 0, 0), (0, 1, 0, width), (1, 0, 0, 2 * width), (1, 1, 1, 0)]
    early_layout = [(0, i * share, share, width, 0, i * width) for i in range(inner // width)]
    early_layout += [(1, 0, mlp_rows, width, 1, 0)]
    early_layout += [
        (half, mlp_rows + index * share, share, width, 2 + out, column)
        for half, index, out, column in attention_layout
    ]
    late_layout = [(half, index * share, share, width, out, column) for half, index, out, column in attention_layout]
    attention_outs = [((share, time_input.shape[1]), F32), ((share, width), F32)]
    mlp_outs = [((share, inner), F32), ((mlp_rows, width), F32)]
    up_grad, down_grad, space_in_grad, space_out_grad = finish(
        packed, core, early_own, early_got, mlp_outs + attention_outs, early_layout, "finish_early"
    )
    time_in_grad, time_out_grad, gains_grad = finish(
        packed, core, late_own, late_got, attention_outs, late_layout, "finish_late", gains=2 * share
    )
    return (
        input_grad,
        time_in_grad,
        time_out_grad,
        space_in_grad,
        space_out_grad,
        up_grad,
        down_grad,
        gains_grad,
    )


def solution(mesh):
    tokens = P(("parts", "clip"), "frame", None, None)
    owned = P(("parts", "frame"), None)
    in_specs = (tokens, tokens) + (P(),) * 7
    out_specs = (tokens,) + (owned,) * 6 + (P("parts", None),)
    return jax.shard_map(body, mesh=mesh, in_specs=in_specs, out_specs=out_specs, check_vma=False)
```
